32 devices in a mesh: dp: 4 (over y, core), fsdp: 4 (over z), tensor: 2 (over x).
Axes of the slice: x: 2, y: 2, z: 4, core: 2. Of those that a mesh axis runs over, the one named last changes fastest.
Arguments:
- tokens: bfloat16 [32, 128, 4096], P(('dp', 'fsdp')), may hold values from -6 to 6
- send_flags: int32 [4, 4], replicated, may hold values from 0 to 1
- doc_lengths: int32 [32, 4], replicated, may hold values from 1 to 64, 128 in all within a row
- cotangent: bfloat16 [32, 128, 8192], P(('dp', 'fsdp')), may hold values from -6 to 6
- w_x: bfloat16 [4096, 8192], P(None, ('fsdp', 'tensor')), may hold values from -0.09375 to 0.09375
- w_z: bfloat16 [4096, 8192], P(None, ('fsdp', 'tensor')), may hold values from -0.09375 to 0.09375
- w_dt: bfloat16 [4096, 128], P(None, ('fsdp', 'tensor')), may hold values from -0.09375 to 0.09375
- w_bc: bfloat16 [4096, 256], replicated, may hold values from -0.09375 to 0.09375
- conv_w: float32 [4, 8192], P(None, ('fsdp', 'tensor')), may hold values from -0.5 to 0.5
- conv_b: float32 [8192], P(('fsdp', 'tensor')), may hold values from -0.5 to 0.5
- norm_gain: float32 [8192], P(('fsdp', 'tensor')), may hold values from 0.5 to 1.5
- a_log: float32 [128], P(('fsdp', 'tensor')), may hold values from 0 to 2.77
- dt_bias: float32 [128], P(('fsdp', 'tensor')), may hold values from -6.9 to -2.3
- skip_scale: float32 [128], P(('fsdp', 'tensor')), may hold values from 0.5 to 1.5
Outputs:
- grad_w_x: float32 [4096, 8192], P('dp', ('fsdp', 'tensor'))
- grad_w_z: float32 [4096, 8192], P('dp', ('fsdp', 'tensor'))
- grad_w_dt: float32 [4096, 128], P('dp', ('fsdp', 'tensor'))
- grad_channel: float32 [6, 8192], P(None, ('fsdp', 'tensor'))
- grad_head: float32 [3, 128], P(None, ('fsdp', 'tensor'))
The draws below stay inside these ranges and needn't reach their ends.
Inputs may be any that keep to these rules, and one draw needn't show every extreme that they name: `send_flags`: each flag is 0 or 1; slots of a device beyond its live count hold values that no output reads. `doc_lengths`: each block's lengths sum to 128, and the largest is exactly 64.
All inputs are finite; a program needn't handle non-finite values.
Results may differ from the reference program's by a relative error of at most 0.009.
Values may be sent and summed in bfloat16 or wider, within the bound.
No kernel may reach another device: no remote copies, remote signals or barrier semaphores. Data moves between devices by JAX's collectives and lax.ppermute only.
A program may use at most 128 MiB of HBM per device.

```python
import math
import jax
import jax.numpy as jnp
import numpy as np
from jax import lax

D = 4096
E = 8192
HEADS = 128
NS = 128
KC = 4
BL = 128
SLOTS = 2
DOCS = 4
NORM_GROUP = 512
RAW_BLOCKS = 32
N_DP = 4
N_FSDP = 4


def set_ends(values, own_key, least, largest):
    longest = values.shape.index(max(values.shape))
    spots = []
    for shift in (0, 1):
        where = [jax.random.randint(jax.random.fold_in(own_key, axis), (), 0, length) for axis, length in enumerate(values.shape)]
        where[longest] = (where[longest] + shift) % values.shape[longest]
        spots.append(tuple(where))
    return values.at[spots[0]].set(least).at[spots[1]].set(largest)


def block_scale(key, dims, split, least, top_value):
    def one(dim, parts):
        draws = jax.random.uniform(jax.random.fold_in(jax.random.fold_in(key, 6), dim), (parts,), jnp.float32, least / len(split), top_value / len(split))
        return jnp.repeat(jnp.exp(draws), dims[dim] // parts).reshape((-1,) + (1,) * (len(dims) - dim - 1))

    loudness = one(*split[0])
    for cut in split[1:]:
        loudness = loudness * one(*cut)
    return loudness


def split_up(count, total, reach, skew):
    weights = [(1 << 20) // math.isqrt(standing ** skew) + 1 for standing in range(2, count + 1)]
    spare, given = total - reach - (count - 1), [1] * (count - 1)
    while spare > 0:
        movable = [i for i in range(count - 1) if given[i] < reach]
        pool, budget = sum([weights[i] for i in movable]), spare
        for i in movable:
            more = min(reach - given[i], max(1, budget * weights[i] // pool), spare)
            given[i] = given[i] + more
            spare = spare - more
    return np.array([reach] + given)


def ragged_sizes(own_key, count, total, most, lean):
    if count == 2:
        one = jax.random.randint(own_key, (), max(1, total - most), min(most, total - 1) + 1)
        return jnp.stack([one, total - one])
    sizes = jnp.asarray(split_up(count, total, most, lean), jnp.int32)
    twos = (count - 1) // 2
    giver, taker = sizes[1:1 + 2 * twos:2], sizes[2:2 + 2 * twos:2]
    slack = jnp.minimum(giver - 1, most - taker)
    moved = jax.random.randint(jax.random.fold_in(own_key, 1), (twos,), 0, 1 << 20) % (slack + 1)
    sizes = sizes.at[1:1 + 2 * twos:2].set(giver - moved).at[2:2 + 2 * twos:2].set(taker + moved)
    return sizes[jax.random.permutation(jax.random.fold_in(own_key, 2), count)]


def gaussian(own_key, shape, width, most, split=(), held_as=jnp.bfloat16):
    gain = block_scale(own_key, shape, split, -0.22, 0.18) if split else 1.0
    values = jax.random.normal(own_key, shape, jnp.float32) * width * gain
    return jnp.minimum(jnp.maximum(values, -most), most).astype(held_as)


def setup_inputs(seed: int = 0) -> dict:
    arg_keys = jax.random.split(jax.random.key(seed), 15)
    return {
        "tokens": gaussian(arg_keys[0], (RAW_BLOCKS, BL, D), 1.0, 6.0, ((0, 16),)),
        "send_flags": set_ends(jax.random.randint(arg_keys[1], (N_DP, N_FSDP), 0, 2), jax.random.fold_in(arg_keys[1], 1), 0, 1).astype(jnp.int32),
        "doc_lengths": jax.vmap(lambda own: ragged_sizes(own, DOCS, BL, BL // 2, 1))(jax.random.split(arg_keys[2], RAW_BLOCKS)).reshape((RAW_BLOCKS, DOCS)).astype(jnp.int32),
        "cotangent": gaussian(arg_keys[3], (RAW_BLOCKS, BL, E), 1.0, 6.0, ((0, 16),)),
        "w_x": gaussian(arg_keys[4], (D, E), D ** -0.5, 0.09375, ((1, 8),)),
        "w_z": gaussian(arg_keys[5], (D, E), D ** -0.5, 0.09375, ((1, 8),)),
        "w_dt": gaussian(arg_keys[6], (D, HEADS), D ** -0.5, 0.09375, ((1, 8),)),
        "w_bc": gaussian(arg_keys[7], (D, 2 * NS), D ** -0.5, 0.09375),
        "conv_w": jnp.clip(jax.random.uniform(arg_keys[8], (KC, E), jnp.float32, -0.5, 0.5) * block_scale(arg_keys[8], (KC, E), ((1, 8),), -0.4, 0.0), -0.5, 0.5),
        "conv_b": jnp.clip(jax.random.uniform(arg_keys[9], (E,), jnp.float32, -0.5, 0.5) * block_scale(arg_keys[9], (E,), ((0, 8),), -0.4, 0.0), -0.5, 0.5),
        "norm_gain": jnp.clip(1.0 + 0.1 * jax.random.normal(arg_keys[10], (E,), jnp.float32), 0.5, 1.5),
        "a_log": jnp.clip(2.77 * jax.random.uniform(arg_keys[11], (HEADS,), jnp.float32) ** block_scale(arg_keys[11], (HEADS,), ((0, 8),), -0.2, 0.2), 0.0, 2.77),
        "dt_bias": jnp.clip(-6.9 + 4.6000001430511475 * jax.random.uniform(arg_keys[12], (HEADS,), jnp.float32) ** block_scale(arg_keys[12], (HEADS,), ((0, 8),), -0.2, 0.2), -6.9, -2.3),
        "skip_scale": jnp.clip(0.5 + 1.0 * jax.random.uniform(arg_keys[13], (HEADS,), jnp.float32) ** block_scale(arg_keys[13], (HEADS,), ((0, 8),), -0.2, 0.2), 0.5, 1.5),
    }


def segment_ids(doc_sizes, block_len):
    doc_ends = jnp.cumsum(doc_sizes, axis=-1, dtype=jnp.int32)[:, :-1]
    positions = jnp.arange(block_len, dtype=jnp.int32)
    return lax.optimization_barrier(jnp.sum((positions[None, :, None] >= doc_ends[:, None, :]).astype(jnp.int32), axis=-1, dtype=jnp.int32))

def gated_ssd(proj_x, proj_z, proj_dt, conv_w, conv_b, norm_gain, a_log, dt_bias, skip_scale, b_mat, c_mat, segments):
    blocks, length, channels = proj_x.shape
    head_count = proj_dt.shape[2]
    tap_count = conv_w.shape[0]
    summed = conv_b + conv_w[tap_count - 1] * proj_x
    for shift_by in range(1, tap_count):
        shifted = jnp.pad(proj_x, ((0, 0), (shift_by, 0), (0, 0)))[:, :length]
        shifted_seg = jnp.pad(segments, ((0, 0), (shift_by, 0)), constant_values=-1)[:, :length]
        summed = summed + conv_w[tap_count - 1 - shift_by] * jnp.where((shifted_seg == segments)[:, :, None], shifted, 0.0)
    inside = jax.nn.silu(summed)
    step_size = jax.nn.softplus(proj_dt + dt_bias)
    decay_rate = -jnp.exp(a_log)
    levels = jnp.cumsum(step_size * decay_rate, axis=1)
    scores = lax.dot_general(c_mat, b_mat, (((2,), (2,)), ((0,), (0,))), preferred_element_type=jnp.float32)
    position = jnp.arange(length)
    causal = (position[:, None] >= position[None, :])[None] & (segments[:, :, None] == segments[:, None, :])
    inside_mask = causal[..., None]
    spread_gap = levels[:, :, None, :] - levels[:, None, :, :]
    decays = jnp.where(inside_mask, jnp.exp(jnp.where(inside_mask, spread_gap, 0.0)), 0.0)
    weights = scores[..., None] * decays * step_size[:, None, :, :]
    heads_in = inside.reshape(blocks, length, head_count, channels // head_count)
    mixed_out = jnp.einsum('bpqh,bqhd->bphd', weights, heads_in, precision=lax.Precision.HIGHEST)
    mixed_out = mixed_out + skip_scale[:, None] * heads_in
    gated = mixed_out.reshape(blocks, length, channels) * jax.nn.silu(proj_z)
    grouped = gated.reshape(blocks, length, channels // NORM_GROUP, NORM_GROUP)
    inv_scale = lax.rsqrt(lax.optimization_barrier(jnp.mean(grouped * grouped, axis=-1, keepdims=True)) + 1e-05)
    return (grouped * inv_scale).reshape(blocks, length, channels) * norm_gain

def local_grads(proj_x, proj_z, proj_dt, params, b_mat, c_mat, segments, cotan):

    def forward(proj_x, proj_z, proj_dt, conv_w, conv_b, norm_gain, a_log, dt_bias, skip_scale):
        return gated_ssd(proj_x, proj_z, proj_dt, conv_w, conv_b, norm_gain, a_log, dt_bias, skip_scale, b_mat, c_mat, segments)
    outputs, pullback = jax.vjp(forward, proj_x, proj_z, proj_dt, *params)
    return pullback(cotan)

def reference(tokens, send_flags, doc_lengths, cotangent, w_x, w_z, w_dt, w_bc, conv_w, conv_b, norm_gain, a_log, dt_bias, skip_scale):
    groups = jnp.arange(N_DP, dtype=jnp.int32)[:, None]
    columns = jnp.arange(N_FSDP, dtype=jnp.int32)[None, :]
    before = (groups + N_DP - 1) % N_DP
    earlier = (groups + N_DP - 2) % N_DP
    came_flag = send_flags[before, columns]
    sent_slot = 1 - send_flags[earlier, columns]
    block_index = jnp.where(came_flag == 1, (before * N_FSDP + columns) * SLOTS + sent_slot, (groups * N_FSDP + columns) * SLOTS).astype(jnp.int32)
    w_in = jnp.concatenate((w_x, w_z, w_dt), axis=1)
    params = (conv_w, conv_b, norm_gain, a_log, dt_bias, skip_scale)

    def one_group(running, block_picks):
        weight_sum, channel_sum, head_sum = running
        x_blocks = tokens[block_picks]
        flat_x = x_blocks.reshape(N_FSDP * BL, D)
        projected = jnp.dot(flat_x, w_in, preferred_element_type=jnp.float32).reshape(N_FSDP, BL, 2 * E + HEADS)
        state_maps = jnp.dot(flat_x, w_bc, preferred_element_type=jnp.float32).astype(jnp.bfloat16)
        state_maps = state_maps.reshape(N_FSDP, BL, 2 * NS)
        segments = segment_ids(doc_lengths[block_picks], BL)
        gradients = local_grads(projected[..., :E], projected[..., E:2 * E], projected[..., 2 * E:], params, state_maps[..., :NS], state_maps[..., NS:], segments, cotangent[block_picks].astype(jnp.float32))
        pre_grad = jnp.concatenate(gradients[:3], axis=-1).astype(jnp.bfloat16).reshape(N_FSDP * BL, 2 * E + HEADS)
        group_part = jnp.dot(flat_x.T, pre_grad, preferred_element_type=jnp.float32)
        group_part = lax.optimization_barrier(group_part.astype(jnp.bfloat16)).astype(jnp.float32)
        channel_grads = jnp.concatenate((gradients[3], gradients[4][None], gradients[5][None]), axis=0)
        head_grads = jnp.stack((gradients[6], gradients[7], gradients[8]))
        return ((weight_sum + group_part, channel_sum + channel_grads, head_sum + head_grads), None)
    starting = (jnp.zeros((D, 2 * E + HEADS), jnp.float32), jnp.zeros((KC + 2, E), jnp.float32), jnp.zeros((3, HEADS), jnp.float32))
    (weight_sum, channel_sum, head_sum), unused = lax.scan(one_group, starting, block_index)
    return (weight_sum[:, :E], weight_sum[:, E:2 * E], weight_sum[:, 2 * E:], channel_sum, head_sum)
```

```python
import jax
import jax.numpy as jnp
from jax import lax
from jax.experimental import pallas as pl
from jax.experimental.pallas import tpu as pltpu
from jax.sharding import PartitionSpec as P

NORM_GROUP = 512
PAIR = 128
CHUNKS = 4
F32 = jnp.float32
BF16 = jnp.bfloat16


def split_two(v):
    hi = v.astype(BF16)
    return hi, (v - hi.astype(F32)).astype(BF16)


def split_three(v):
    hi = v.astype(BF16)
    rest = v - hi.astype(F32)
    mid = rest.astype(BF16)
    return hi, mid, (rest - mid.astype(F32)).astype(BF16)


def dot_nn(a, b):
    return lax.dot_general(a, b, (((1,), (0,)), ((), ())), preferred_element_type=F32)


def dot_nt(a, b):
    return lax.dot_general(a, b, (((1,), (1,)), ((), ())), preferred_element_type=F32)


def dot_tn(a, b):
    return lax.dot_general(a, b, (((0,), (0,)), ((), ())), preferred_element_type=F32)


def exact_rows(rows, ones):
    n = rows.shape[0]
    got = dot_nn(jnp.concatenate(split_three(rows), axis=0), ones)
    return got[:n] + got[n : 2 * n] + got[2 * n :]


def scan_kernel(
    ends_ref, px_ref, pz_ref, pdt_ref, cot_ref, bc_ref,
    cw_ref, cb_ref, gain_ref, skipc_ref, alog_ref, dtb_ref,
    gpre_ref, gpdt_ref, gch_ref, gh_ref,
):
    block = pl.program_id(1)
    length = px_ref.shape[1]
    group = px_ref.shape[2]
    taps = cw_ref.shape[0]
    states = bc_ref.shape[2] // 2
    heads = pdt_ref.shape[2]
    head_dim = group // heads
    pairs = group // PAIR
    docs = ends_ref.shape[1]

    row = lax.broadcasted_iota(jnp.int32, (length, length), 0)
    col = lax.broadcasted_iota(jnp.int32, (length, length), 1)
    start_row = jnp.zeros((length, length), jnp.int32)
    start_col = jnp.zeros((length, length), jnp.int32)
    for k in range(docs):
        end = ends_ref[block, k]
        start_row = jnp.where(row >= end, end, start_row)
        start_col = jnp.where(col >= end, end, start_col)
    inside = (row >= col) & (start_row == start_col)
    offset = (row - start_row)[:, :PAIR]
    near = [None] + [(offset >= j).astype(F32) for j in range(1, taps)]
    low = lax.broadcasted_iota(jnp.int32, (length, PAIR), 1) < head_dim
    upto = (row <= col).astype(BF16)

    bmat = bc_ref[0, :, :states]
    cmat = bc_ref[0, :, states:]
    scores = dot_nt(cmat, bmat)

    decay = -jnp.exp(alog_ref[0])
    raw = pdt_ref[0, 0] + dtb_ref[0]
    soft = jnp.exp(-jnp.abs(raw))
    step = jnp.maximum(raw, 0.0) + jnp.log1p(soft)
    dstep = jnp.where(raw >= 0.0, 1.0, soft) / (1.0 + soft)
    level = exact_rows(step * decay, upto)
    both = jnp.concatenate(
        [step, level, jnp.zeros((length - 2 * heads, length), F32)], axis=0
    ).T

    kept = []
    square_sum = jnp.zeros((length, PAIR), F32)
    cross_sum = jnp.zeros((length, PAIR), F32)
    for k in range(pairs):
        at = slice(k * PAIR, (k + 1) * PAIR)
        x = px_ref[0, :, at]
        back = [x] + [near[j] * pltpu.roll(x, j, 0) for j in range(1, taps)]
        s = cb_ref[:, at]
        for j in range(taps):
            s = s + cw_ref[taps - 1 - j : taps - j, at] * back[j]
        sig = jax.nn.sigmoid(s)
        u = s * sig
        dsilu = sig * (1.0 + s * (1.0 - sig))
        spread = []
        for h in (2 * k, 2 * k + 1):
            gap = both[:, heads + h : heads + h + 1] - level[h : h + 1, :]
            spread.append((jnp.exp(jnp.where(inside, gap, -1e30)) * scores).astype(BF16))
        step_wide = jnp.where(low, both[:, 2 * k : 2 * k + 1], both[:, 2 * k + 1 : 2 * k + 2])
        ud = (step_wide * u).astype(BF16).astype(F32)
        zero = jnp.zeros_like(ud)
        udc = jnp.concatenate([jnp.where(low, ud, zero), jnp.where(low, zero, ud)], axis=0).astype(BF16)
        mix = dot_nn(jnp.concatenate(spread, axis=1), udc)
        y = mix + skipc_ref[:, at] * u
        z = pz_ref[0, :, at]
        zsig = jax.nn.sigmoid(z)
        zs = z * zsig
        v = y * zs
        dn = cot_ref[0, :, at].astype(F32) * gain_ref[:, at]
        square_sum = square_sum + v * v
        cross_sum = cross_sum + dn * v
        kept.append((back, u, ud, dsilu, jnp.concatenate(spread, axis=0), step_wide, mix, y, z, zsig, zs, v, dn))

    inv = lax.rsqrt(jnp.sum(square_sum, axis=1, keepdims=True) * (1.0 / group) + 1e-05)
    lean = inv * inv * jnp.sum(cross_sum, axis=1, keepdims=True) * (1.0 / group)

    channel_rows = []
    use_parts = []
    mix_parts = []
    skip_parts = []
    for k in range(pairs):
        at = slice(k * PAIR, (k + 1) * PAIR)
        back, u, ud, dsilu, spread, step_wide, mix, y, z, zsig, zs, v, dn = kept[k]
        dgain = jnp.sum(cot_ref[0, :, at].astype(F32) * (v * inv), axis=0, keepdims=True)
        dv = inv * (dn - v * lean)
        dy = dv * zs
        dz = dv * y * (zsig * (1.0 + z * (1.0 - zsig)))
        gpre_ref[1, 0, :, at] = dz.astype(BF16)
        dyr = dy.astype(BF16).astype(F32)
        zero = jnp.zeros_like(dy)
        dyc = jnp.concatenate([jnp.where(low, dyr, zero), jnp.where(low, zero, dyr)], axis=0).astype(BF16)
        turned = dot_tn(spread, dyc)
        du = step_wide * turned + skipc_ref[:, at] * dy
        use_parts.append(u * turned)
        mix_parts.append(dyr * mix - ud * turned)
        skip_parts.append(jnp.sum(dy * u, axis=0, keepdims=True))
        ds = du * dsilu
        rows = []
        dx = cw_ref[taps - 1 : taps, at] * ds
        for j in range(taps - 1, 0, -1):
            rows.append(jnp.sum(ds * back[j], axis=0, keepdims=True))
            dx = dx + cw_ref[taps - 1 - j : taps - j, at] * pltpu.roll(near[j] * ds, length - j, 0)
        rows.append(jnp.sum(ds * back[0], axis=0, keepdims=True))
        rows.append(jnp.sum(ds, axis=0, keepdims=True))
        rows.append(dgain)
        gpre_ref[0, 0, :, at] = dx.astype(BF16)
        channel_rows.append(jnp.concatenate(rows, axis=0))
    channel = jnp.concatenate(channel_rows, axis=1)

    of_head = (
        lax.broadcasted_iota(jnp.int32, (heads, group), 1) // head_dim
        == lax.broadcasted_iota(jnp.int32, (heads, group), 0)
    ).astype(BF16)
    use_hi, use_lo = split_two(jnp.concatenate(use_parts, axis=1))
    use_sum = dot_nt(of_head, use_hi) + dot_nt(of_head, use_lo)
    mix_hi, mix_lo = split_two(jnp.concatenate(mix_parts, axis=1))
    mix_sum = dot_nt(of_head, mix_hi) + dot_nt(of_head, mix_lo)
    after = exact_rows(mix_sum, (row >= col).astype(BF16))
    dalog = jnp.sum(step * after, axis=1, keepdims=True) * decay
    draw = (use_sum + decay * after) * dstep
    gpdt_ref[0, 0] = draw
    ddtb = jnp.sum(draw, axis=1, keepdims=True)
    skip_row = jnp.concatenate(skip_parts, axis=1)
    dskip = jnp.sum(jnp.where(of_head > 0, skip_row, 0.0), axis=1, keepdims=True)
    head = jnp.concatenate([dalog, ddtb, dskip], axis=1)

    @pl.when(block == 0)
    def _():
        gch_ref[...] = channel
        gh_ref[0] = head

    @pl.when(block > 0)
    def _():
        gch_ref[...] += channel
        gh_ref[0] += head


def scan_backward(ends, px, pz, pdt, cot, bc, conv_w, conv_b, norm_gain, skip_chan, a_log, dt_bias):
    blocks, length, channels = px.shape
    groups, _, heads, _ = pdt.shape
    taps = conv_w.shape[0]
    wide = channels // groups
    per_block = pl.BlockSpec((1, length, wide), lambda g, b: (b, 0, g))
    per_group = lambda rows: pl.BlockSpec((rows, wide), lambda g, b: (0, g))
    head_spec = pl.BlockSpec((1, heads, 1), lambda g, b: (g, 0, 0))
    return pl.pallas_call(
        scan_kernel,
        grid=(groups, blocks),
        in_specs=[
            pl.BlockSpec(memory_space=pltpu.SMEM),
            per_block, per_block,
            pl.BlockSpec((1, 1, heads, length), lambda g, b: (g, b, 0, 0)),
            per_block,
            pl.BlockSpec((1, length, bc.shape[2]), lambda g, b: (b, 0, 0)),
            per_group(taps), per_group(1), per_group(1), per_group(1),
            head_spec, head_spec,
        ],
        out_specs=[
            pl.BlockSpec((2, 1, length, wide), lambda g, b: (0, b, 0, g)),
            pl.BlockSpec((1, 1, heads, length), lambda g, b: (g, b, 0, 0)),
            per_group(taps + 2),
            pl.BlockSpec((1, heads, 3), lambda g, b: (g, 0, 0)),
        ],
        out_shape=[
            jax.ShapeDtypeStruct((2, blocks, length, channels), BF16),
            jax.ShapeDtypeStruct(pdt.shape, F32),
            jax.ShapeDtypeStruct((taps + 2, channels), F32),
            jax.ShapeDtypeStruct((groups, heads, 3), F32),
        ],
        compiler_params=pltpu.CompilerParams(vmem_limit_bytes=32 * 2**20),
        cost_estimate=pl.CostEstimate(
            flops=400 * blocks * length * channels,
            bytes_accessed=18 * blocks * length * channels,
            transcendentals=10 * blocks * length * channels,
        ),
    )(
        ends, px, pz, pdt, cot, bc, conv_w, conv_b[None], norm_gain[None], skip_chan[None],
        a_log.reshape(groups, heads, 1), dt_bias.reshape(groups, heads, 1),
    )


def xor_pairs(size, by):
    return [(i, i ^ by) for i in range(size)]


def shifted(shard, axis, by):
    size = lax.axis_size(axis)
    return lax.ppermute(shard, axis, [(i, (i + by) % size) for i in range(size)])


def swapped(shard, axis, by):
    return lax.ppermute(shard, axis, xor_pairs(lax.axis_size(axis), by))


def tree_sum(parts):
    while len(parts) > 1:
        parts = [a + b for a, b in zip(parts[0::2], parts[1::2], strict=True)]
    return parts[0]


def per_device(
    tokens,
    send_flags,
    doc_lengths,
    cotangent,
    w_x,
    w_z,
    w_dt,
    w_bc,
    conv_w,
    conv_b,
    norm_gain,
    a_log,
    dt_bias,
    skip_scale,
):
    dp_count = lax.axis_size("dp")
    fsdp_count = lax.axis_size("fsdp")
    pair_count = lax.axis_size("tensor")
    dp_index = lax.axis_index("dp")
    column = lax.axis_index("fsdp")
    member = lax.axis_index("tensor")
    slots, length, width = tokens.shape
    half = length // pair_count
    chan = w_x.shape[1]
    head_count = w_dt.shape[1]
    groups = chan // NORM_GROUP
    taps = conv_w.shape[0]
    piece = width // dp_count
    zero = jnp.zeros((), jnp.int32)

    before = (dp_index + dp_count - 1) % dp_count
    earlier = (dp_index + dp_count - 2) % dp_count
    came = send_flags[before, column] == 1
    own_send = 1 - send_flags[before, column]

    def in_order(mine, other):
        return jnp.where(
            member == 0,
            jnp.concatenate((mine, other), axis=0),
            jnp.concatenate((other, mine), axis=0),
        )

    halves = []
    for which in (member, 1 - member):
        here = (zero, which * half, zero)
        there = (own_send, which * half, zero)
        got = shifted(lax.dynamic_slice(tokens, there, (1, half, width))[0], "dp", 1)
        halves.append(jnp.where(came, got, lax.dynamic_slice(tokens, here, (1, half, width))[0]))
    x_blocks = [in_order(halves[0], halves[1])]
    for k in range(1, fsdp_count):
        got = swapped(halves[0], "fsdp", k)
        x_blocks.append(in_order(got, swapped(got, "tensor", 1)))

    def slabs(slot):
        rows = lax.dynamic_index_in_dim(cotangent, slot, 0, keepdims=False)
        rows = rows.reshape(length, fsdp_count, pair_count, chan)
        rows = lax.dynamic_index_in_dim(rows, member, 2, keepdims=False)
        return rows.transpose(1, 0, 2)

    mine_d = jnp.where(came, shifted(slabs(own_send), "dp", 1), slabs(zero))
    d_blocks = []
    for k in range(fsdp_count):
        part = lax.dynamic_index_in_dim(mine_d, column ^ k, 0, keepdims=False)
        d_blocks.append(swapped(part, "fsdp", k) if k else part)

    columns = column ^ jnp.arange(fsdp_count, dtype=jnp.int32)
    picks = jnp.where(
        send_flags[before][columns] == 1,
        (before * fsdp_count + columns) * slots + 1 - send_flags[earlier][columns],
        (dp_index * fsdp_count + columns) * slots,
    )
    sizes = doc_lengths[picks]
    ends = [sizes[:, 0]]
    for k in range(1, sizes.shape[1] - 1):
        ends.append(ends[-1] + sizes[:, k])
    ends = jnp.stack(ends, axis=1)
    skip_chan = jnp.repeat(skip_scale, chan // head_count)

    per_chunk = max(1, fsdp_count // CHUNKS)
    x_parts = [[] for _ in range(dp_count)]
    g_parts = [[] for _ in range(dp_count)]
    dt_parts = []
    channel_parts = []
    head_parts = []
    for first in range(0, fsdp_count, per_chunk):
        last = first + per_chunk
        xs = jnp.concatenate(x_blocks[first:last], axis=0)
        cot = jnp.stack(d_blocks[first:last])
        px = jnp.dot(xs, w_x, preferred_element_type=F32).reshape(per_chunk, length, chan)
        pz = jnp.dot(xs, w_z, preferred_element_type=F32).reshape(per_chunk, length, chan)
        bc = jnp.dot(xs, w_bc, preferred_element_type=F32).astype(BF16)
        bc = bc.reshape(per_chunk, length, w_bc.shape[1])
        pdt = lax.dot_general(w_dt, xs, (((0,), (1,)), ((), ())), preferred_element_type=F32)
        pdt = pdt.reshape(groups, head_count // groups, per_chunk, length).transpose(0, 2, 1, 3)
        gpre, gpdt, gch, gh = scan_backward(
            ends[first:last], px, pz, pdt, cot, bc,
            conv_w, conv_b, norm_gain, skip_chan, a_log, dt_bias,
        )
        dt_parts.append(gpdt.transpose(1, 0, 2, 3).reshape(per_chunk, head_count, length))
        channel_parts.append(gch)
        head_parts.append(gh)
        gpre = gpre.reshape(2, per_chunk * length, chan)
        for m in range(0, dp_count, 2):
            got = swapped(gpre, "dp", m) if m else gpre
            g_parts[m].append(got)
            g_parts[m + 1].append(swapped(got, "dp", 1))
        for m in range(dp_count):
            part = lax.dynamic_slice(xs, (zero, (dp_index ^ m) * piece), (xs.shape[0], piece))
            x_parts[m].append(swapped(part, "dp", m) if m else part)

    gpdt = jnp.concatenate(dt_parts, axis=0).reshape(-1, chan)
    rows = [gpdt, sum(channel_parts[1:], channel_parts[0])]
    heads = sum(head_parts[1:], head_parts[0]).reshape(head_count, 3).T
    rows.append(jnp.pad(heads.reshape(1, -1), ((0, 0), (0, chan - 3 * head_count))))
    packed = jnp.concatenate(rows, axis=0)
    packs = [packed if m == 0 else swapped(packed, "dp", m) for m in range(dp_count)]
    dt_rows = gpdt.shape[0]
    small = tree_sum([p[dt_rows:] for p in packs])
    channel_sum = small[: taps + 2]
    head_sum = small[taps + 2, : 3 * head_count].reshape(3, head_count)

    def product(ms, which):
        x_all = jnp.concatenate([p for m in ms for p in x_parts[m]], axis=0)
        g_all = jnp.concatenate([p[which] for m in ms for p in g_parts[m]], axis=0)
        return lax.dot_general(x_all, g_all, (((0,), (0,)), ((), ())), preferred_element_type=F32)

    near = tuple(range(2))
    far = tuple(range(2, dp_count))
    grad_x = product(near, 0) + product(far, 0)
    grad_z = product(near, 1) + product(far, 1)
    x_all = jnp.concatenate([p for parts in x_parts for p in parts], axis=0)
    dt_all = jnp.concatenate([p[:dt_rows].reshape(-1, head_count, length) for p in packs], axis=0)
    dt_all = dt_all.astype(BF16).transpose(1, 0, 2).reshape(head_count, -1)
    grad_dt = lax.dot_general(x_all, dt_all, (((0,), (1,)), ((), ())), preferred_element_type=F32)
    return grad_x, grad_z, grad_dt, channel_sum, head_sum


def solution(mesh):
    split = ("fsdp", "tensor")
    placed = (
        P(("dp", "fsdp"), None, None),
        P(),
        P(),
        P(("dp", "fsdp"), None, None),
        P(None, split),
        P(None, split),
        P(None, split),
        P(),
        P(None, split),
        P(split),
        P(split),
        P(split),
        P(split),
        P(split),
    )
    return jax.shard_map(
        per_device,
        mesh=mesh,
        in_specs=placed,
        out_specs=(P("dp", split), P("dp", split), P("dp", split), P(None, split), P(None, split)),
        check_vma=False,
    )
```

```python
import jax
import jax.numpy as jnp
from jax import lax
from jax.experimental import pallas as pl
from jax.experimental.pallas import tpu as pltpu
from jax.sharding import PartitionSpec as P

NORM_GROUP = 512
PAIR = 128
CHUNKS = 2
F32 = jnp.float32
BF16 = jnp.bfloat16


def split_two(v):
    hi = v.astype(BF16)
    return hi, (v - hi.astype(F32)).astype(BF16)


def split_three(v):
    hi = v.astype(BF16)
    rest = v - hi.astype(F32)
    mid = rest.astype(BF16)
    return hi, mid, (rest - mid.astype(F32)).astype(BF16)


def dot_nn(a, b):
    return lax.dot_general(a, b, (((1,), (0,)), ((), ())), preferred_element_type=F32)


def dot_nt(a, b):
    return lax.dot_general(a, b, (((1,), (1,)), ((), ())), preferred_element_type=F32)


def dot_tn(a, b):
    return lax.dot_general(a, b, (((0,), (0,)), ((), ())), preferred_element_type=F32)


def exact_rows(rows, ones):
    n = rows.shape[0]
    got = dot_nn(jnp.concatenate(split_three(rows), axis=0), ones)
    return got[:n] + got[n : 2 * n] + got[2 * n :]


def scan_kernel(
    ends_ref, px_ref, pz_ref, pdt_ref, cot_ref, bc_ref,
    cw_ref, cb_ref, gain_ref, skipc_ref, alog_ref, dtb_ref,
    gpre_ref, gpdt_ref, gch_ref, gh_ref,
):
    block = pl.program_id(1)
    length = px_ref.shape[1]
    group = px_ref.shape[2]
    taps = cw_ref.shape[0]
    states = bc_ref.shape[2] // 2
    heads = pdt_ref.shape[2]
    head_dim = group // heads
    pairs = group // PAIR
    docs = ends_ref.shape[1]

    row = lax.broadcasted_iota(jnp.int32, (length, length), 0)
    col = lax.broadcasted_iota(jnp.int32, (length, length), 1)
    start_row = jnp.zeros((length, length), jnp.int32)
    start_col = jnp.zeros((length, length), jnp.int32)
    for k in range(docs):
        end = ends_ref[block, k]
        start_row = jnp.where(row >= end, end, start_row)
        start_col = jnp.where(col >= end, end, start_col)
    inside = (row >= col) & (start_row == start_col)
    offset = (row - start_row)[:, :PAIR]
    near = [None] + [(offset >= j).astype(F32) for j in range(1, taps)]
    low = lax.broadcasted_iota(jnp.int32, (length, PAIR), 1) < head_dim
    upto = (row <= col).astype(BF16)

    bmat = bc_ref[0, :, :states]
    cmat = bc_ref[0, :, states:]
    scores = dot_nt(cmat, bmat)

    decay = -jnp.exp(alog_ref[0])
    raw = pdt_ref[0, 0] + dtb_ref[0]
    soft = jnp.exp(-jnp.abs(raw))
    step = jnp.maximum(raw, 0.0) + jnp.log1p(soft)
    dstep = jnp.where(raw >= 0.0, 1.0, soft) / (1.0 + soft)
    level = exact_rows(step * decay, upto)
    both = jnp.concatenate(
        [step, level, jnp.zeros((length - 2 * heads, length), F32)], axis=0
    ).T

    kept = []
    square_sum = jnp.zeros((length, PAIR), F32)
    cross_sum = jnp.zeros((length, PAIR), F32)
    for k in range(pairs):
        at = slice(k * PAIR, (k + 1) * PAIR)
        x = px_ref[0, :, at]
        back = [x] + [near[j] * pltpu.roll(x, j, 0) for j in range(1, taps)]
        s = cb_ref[:, at]
        for j in range(taps):
            s = s + cw_ref[taps - 1 - j : taps - j, at] * back[j]
        sig = jax.nn.sigmoid(s)
        u = s * sig
        dsilu = sig * (1.0 + s * (1.0 - sig))
        spread = []
        for h in (2 * k, 2 * k + 1):
            gap = both[:, heads + h : heads + h + 1] - level[h : h + 1, :]
            spread.append((jnp.exp(jnp.where(inside, gap, -1e30)) * scores).astype(BF16))
        step_wide = jnp.where(low, both[:, 2 * k : 2 * k + 1], both[:, 2 * k + 1 : 2 * k + 2])
        ud = (step_wide * u).astype(BF16).astype(F32)
        zero = jnp.zeros_like(ud)
        udc = jnp.concatenate([jnp.where(low, ud, zero), jnp.where(low, zero, ud)], axis=0).astype(BF16)
        mix = dot_nn(jnp.concatenate(spread, axis=1), udc)
        y = mix + skipc_ref[:, at] * u
        z = pz_ref[0, :, at]
        zsig = jax.nn.sigmoid(z)
        zs = z * zsig
        v = y * zs
        dn = cot_ref[0, :, at].astype(F32) * gain_ref[:, at]
        square_sum = square_sum + v * v
        cross_sum = cross_sum + dn * v
        kept.append((back, u, ud, dsilu, jnp.concatenate(spread, axis=0), step_wide, mix, y, z, zsig, zs, v, dn))

    inv = lax.rsqrt(jnp.sum(square_sum, axis=1, keepdims=True) * (1.0 / group) + 1e-05)
    lean = inv * inv * jnp.sum(cross_sum, axis=1, keepdims=True) * (1.0 / group)

    channel_rows = []
    use_parts = []
    mix_parts = []
    skip_parts = []
    for k in range(pairs):
        at = slice(k * PAIR, (k + 1) * PAIR)
        back, u, ud, dsilu, spread, step_wide, mix, y, z, zsig, zs, v, dn = kept[k]
        dgain = jnp.sum(cot_ref[0, :, at].astype(F32) * (v * inv), axis=0, keepdims=True)
        dv = inv * (dn - v * lean)
        dy = dv * zs
        dz = dv * y * (zsig * (1.0 + z * (1.0 - zsig)))
        gpre_ref[1, 0, :, at] = dz.astype(BF16)
        dyr = dy.astype(BF16).astype(F32)
        zero = jnp.zeros_like(dy)
        dyc = jnp.concatenate([jnp.where(low, dyr, zero), jnp.where(low, zero, dyr)], axis=0).astype(BF16)
        turned = dot_tn(spread, dyc)
        du = step_wide * turned + skipc_ref[:, at] * dy
        use_parts.append(u * turned)
        mix_parts.append(dyr * mix - ud * turned)
        skip_parts.append(jnp.sum(dy * u, axis=0, keepdims=True))
        ds = du * dsilu
        rows = []
        dx = cw_ref[taps - 1 : taps, at] * ds
        for j in range(taps - 1, 0, -1):
            rows.append(jnp.sum(ds * back[j], axis=0, keepdims=True))
            dx = dx + cw_ref[taps - 1 - j : taps - j, at] * pltpu.roll(near[j] * ds, length - j, 0)
        rows.append(jnp.sum(ds * back[0], axis=0, keepdims=True))
        rows.append(jnp.sum(ds, axis=0, keepdims=True))
        rows.append(dgain)
        gpre_ref[0, 0, :, at] = dx.astype(BF16)
        channel_rows.append(jnp.concatenate(rows, axis=0))
    channel = jnp.concatenate(channel_rows, axis=1)

    of_head = (
        lax.broadcasted_iota(jnp.int32, (heads, group), 1) // head_dim
        == lax.broadcasted_iota(jnp.int32, (heads, group), 0)
    ).astype(BF16)
    use_hi, use_lo = split_two(jnp.concatenate(use_parts, axis=1))
    use_sum = dot_nt(of_head, use_hi) + dot_nt(of_head, use_lo)
    mix_hi, mix_lo = split_two(jnp.concatenate(mix_parts, axis=1))
    mix_sum = dot_nt(of_head, mix_hi) + dot_nt(of_head, mix_lo)
    after = exact_rows(mix_sum, (row >= col).astype(BF16))
    dalog = jnp.sum(step * after, axis=1, keepdims=True) * decay
    draw = (use_sum + decay * after) * dstep
    gpdt_ref[0, 0] = draw
    ddtb = jnp.sum(draw, axis=1, keepdims=True)
    skip_row = jnp.concatenate(skip_parts, axis=1)
    dskip = jnp.sum(jnp.where(of_head > 0, skip_row, 0.0), axis=1, keepdims=True)
    head = jnp.concatenate([dalog, ddtb, dskip], axis=1)

    @pl.when(block == 0)
    def _():
        gch_ref[...] = channel
        gh_ref[0] = head

    @pl.when(block > 0)
    def _():
        gch_ref[...] += channel
        gh_ref[0] += head


def scan_backward(ends, px, pz, pdt, cot, bc, conv_w, conv_b, norm_gain, skip_chan, a_log, dt_bias):
    blocks, length, channels = px.shape
    groups, _, heads, _ = pdt.shape
    taps = conv_w.shape[0]
    wide = channels // groups
    per_block = pl.BlockSpec((1, length, wide), lambda g, b: (b, 0, g))
    per_group = lambda rows: pl.BlockSpec((rows, wide), lambda g, b: (0, g))
    head_spec = pl.BlockSpec((1, heads, 1), lambda g, b: (g, 0, 0))
    return pl.pallas_call(
        scan_kernel,
        grid=(groups, blocks),
        in_specs=[
            pl.BlockSpec(memory_space=pltpu.SMEM),
            per_block, per_block,
            pl.BlockSpec((1, 1, heads, length), lambda g, b: (g, b, 0, 0)),
            per_block,
            pl.BlockSpec((1, length, bc.shape[2]), lambda g, b: (b, 0, 0)),
            per_group(taps), per_group(1), per_group(1), per_group(1),
            head_spec, head_spec,
        ],
        out_specs=[
            pl.BlockSpec((2, 1, length, wide), lambda g, b: (0, b, 0, g)),
            pl.BlockSpec((1, 1, heads, length), lambda g, b: (g, b, 0, 0)),
            per_group(taps + 2),
            pl.BlockSpec((1, heads, 3), lambda g, b: (g, 0, 0)),
        ],
        out_shape=[
            jax.ShapeDtypeStruct((2, blocks, length, channels), BF16),
            jax.ShapeDtypeStruct(pdt.shape, F32),
            jax.ShapeDtypeStruct((taps + 2, channels), F32),
            jax.ShapeDtypeStruct((groups, heads, 3), F32),
        ],
        compiler_params=pltpu.CompilerParams(vmem_limit_bytes=32 * 2**20),
        cost_estimate=pl.CostEstimate(
            flops=400 * blocks * length * channels,
            bytes_accessed=18 * blocks * length * channels,
            transcendentals=10 * blocks * length * channels,
        ),
    )(
        ends, px, pz, pdt, cot, bc, conv_w, conv_b[None], norm_gain[None], skip_chan[None],
        a_log.reshape(groups, heads, 1), dt_bias.reshape(groups, heads, 1),
    )


def xor_pairs(size, by):
    return [(i, i ^ by) for i in range(size)]


def shifted(shard, axis, by):
    size = lax.axis_size(axis)
    return lax.ppermute(shard, axis, [(i, (i + by) % size) for i in range(size)])


def swapped(shard, axis, by):
    return lax.ppermute(shard, axis, xor_pairs(lax.axis_size(axis), by))


def after(value, *others):
    return lax.optimization_barrier((value, *others))[0]


def tree_sum(parts):
    while len(parts) > 1:
        parts = [a + b for a, b in zip(parts[0::2], parts[1::2], strict=True)]
    return parts[0]


def per_device(
    tokens,
    send_flags,
    doc_lengths,
    cotangent,
    w_x,
    w_z,
    w_dt,
    w_bc,
    conv_w,
    conv_b,
    norm_gain,
    a_log,
    dt_bias,
    skip_scale,
):
    dp_count = lax.axis_size("dp")
    fsdp_count = lax.axis_size("fsdp")
    pair_count = lax.axis_size("tensor")
    dp_index = lax.axis_index("dp")
    column = lax.axis_index("fsdp")
    member = lax.axis_index("tensor")
    slots, length, width = tokens.shape
    half = length // pair_count
    chan = w_x.shape[1]
    head_count = w_dt.shape[1]
    groups = chan // NORM_GROUP
    taps = conv_w.shape[0]
    piece = width // dp_count
    zero = jnp.zeros((), jnp.int32)

    before = (dp_index + dp_count - 1) % dp_count
    earlier = (dp_index + dp_count - 2) % dp_count
    came = send_flags[before, column] == 1
    own_send = 1 - send_flags[before, column]

    def in_order(mine, other):
        first = jnp.where(member == 0, mine, other)
        second = jnp.where(member == 0, other, mine)
        return jnp.concatenate((first, second), axis=-2)

    def across(own):
        held = [own]
        for k in range(1, fsdp_count):
            low = k & -k
            held.append(swapped(held[k ^ low], "fsdp", low))
        return held

    def half_rows(slot):
        return lax.dynamic_slice(tokens, (slot, member * half, zero), (1, half, width))[0]

    mine_x = jnp.where(came, shifted(half_rows(own_send), "dp", 1), half_rows(zero))
    mine = across(mine_x)
    x_blocks = [in_order(part, swapped(part, "tensor", 1)) for part in mine]

    held_d = after(cotangent, mine_x)

    def slabs(slot):
        return jnp.stack(
            [
                lax.dynamic_slice(held_d, (slot, zero, (f * pair_count + member) * chan), (1, length, chan))[0]
                for f in range(fsdp_count)
            ]
        )

    mine_d = jnp.where(came, shifted(slabs(own_send), "dp", 1), slabs(zero))
    d_blocks = []
    for k in range(fsdp_count):
        part = lax.dynamic_index_in_dim(mine_d, column ^ k, 0, keepdims=False)
        d_blocks.append(swapped(part, "fsdp", k) if k else part)

    def columns_for(rows, m):
        at = (zero,) * (rows.ndim - 1) + ((dp_index ^ m) * piece,)
        return lax.dynamic_slice(rows, at, rows.shape[:-1] + (piece,))

    held_x = after(mine_x, mine_d)
    far_x = jnp.stack([swapped(columns_for(held_x, m), "dp", m) for m in range(2, dp_count)])
    far_x = after(far_x, d_blocks[-1], mine[-1])
    far_x = jnp.stack(across(far_x))
    far_x = in_order(far_x, swapped(far_x, "tensor", 1))

    columns = column ^ jnp.arange(fsdp_count, dtype=jnp.int32)
    picks = jnp.where(
        send_flags[before][columns] == 1,
        (before * fsdp_count + columns) * slots + 1 - send_flags[earlier][columns],
        (dp_index * fsdp_count + columns) * slots,
    )
    sizes = doc_lengths[picks]
    ends = [sizes[:, 0]]
    for k in range(1, sizes.shape[1] - 1):
        ends.append(ends[-1] + sizes[:, k])
    ends = jnp.stack(ends, axis=1)
    skip_chan = jnp.repeat(skip_scale, chan // head_count)

    per_chunk = max(1, fsdp_count // CHUNKS)
    x_parts = [[] for _ in range(dp_count)]
    g_parts = [[] for _ in range(dp_count)]
    dt_parts = []
    channel_parts = []
    head_parts = []
    for first in range(0, fsdp_count, per_chunk):
        last = first + per_chunk
        xs = jnp.concatenate(x_blocks[first:last], axis=0)
        cot = jnp.stack(d_blocks[first:last])
        px = jnp.dot(xs, w_x, preferred_element_type=F32).reshape(per_chunk, length, chan)
        pz = jnp.dot(xs, w_z, preferred_element_type=F32).reshape(per_chunk, length, chan)
        bc = jnp.dot(xs, w_bc, preferred_element_type=F32).astype(BF16)
        bc = bc.reshape(per_chunk, length, w_bc.shape[1])
        pdt = lax.dot_general(w_dt, xs, (((0,), (1,)), ((), ())), preferred_element_type=F32)
        pdt = pdt.reshape(groups, head_count // groups, per_chunk, length).transpose(0, 2, 1, 3)
        gpre, gpdt, gch, gh = scan_backward(
            ends[first:last], px, pz, pdt, cot, bc,
            conv_w, conv_b, norm_gain, skip_chan, a_log, dt_bias,
        )
        dt_parts.append(gpdt.transpose(1, 0, 2, 3).reshape(per_chunk, head_count, length))
        channel_parts.append(gch)
        head_parts.append(gh)
        gpre = gpre.reshape(2, per_chunk * length, chan)
        for m in range(0, dp_count, 2):
            got = swapped(gpre, "dp", m) if m else gpre
            g_parts[m].append(got)
            g_parts[m + 1].append(swapped(got, "dp", 1))
        x_parts[0].append(columns_for(xs, 0))
        x_parts[1].append(swapped(columns_for(xs, 1), "dp", 1))
        for m in range(2, dp_count):
            x_parts[m].append(far_x[first:last, m - 2].reshape(-1, piece))

    gpdt = jnp.concatenate(dt_parts, axis=0).reshape(-1, chan)
    rows = [gpdt, sum(channel_parts[1:], channel_parts[0])]
    heads = sum(head_parts[1:], head_parts[0]).reshape(head_count, 3).T
    rows.append(jnp.pad(heads.reshape(1, -1), ((0, 0), (0, chan - 3 * head_count))))
    packed = jnp.concatenate(rows, axis=0)
    packs = [packed if m == 0 else swapped(packed, "dp", m) for m in range(dp_count)]
    dt_rows = gpdt.shape[0]
    small = tree_sum([p[dt_rows:] for p in packs])
    channel_sum = small[: taps + 2]
    head_sum = small[taps + 2, : 3 * head_count].reshape(3, head_count)

    def product(ms, which):
        x_all = jnp.concatenate([p for m in ms for p in x_parts[m]], axis=0)
        g_all = jnp.concatenate([p[which] for m in ms for p in g_parts[m]], axis=0)
        return lax.dot_general(x_all, g_all, (((0,), (0,)), ((), ())), preferred_element_type=F32)

    near = tuple(range(2))
    far = tuple(range(2, dp_count))
    grad_x = product(near, 0) + product(far, 0)
    grad_z = product(near, 1) + product(far, 1)
    x_all = jnp.concatenate([p for parts in x_parts for p in parts], axis=0)
    dt_all = jnp.concatenate([p[:dt_rows].reshape(-1, head_count, length) for p in packs], axis=0)
    dt_all = dt_all.astype(BF16).transpose(1, 0, 2).reshape(head_count, -1)
    grad_dt = lax.dot_general(x_all, dt_all, (((0,), (1,)), ((), ())), preferred_element_type=F32)
    return grad_x, grad_z, grad_dt, channel_sum, head_sum


def solution(mesh):
    split = ("fsdp", "tensor")
    placed = (
        P(("dp", "fsdp"), None, None),
        P(),
        P(),
        P(("dp", "fsdp"), None, None),
        P(None, split),
        P(None, split),
        P(None, split),
        P(),
        P(None, split),
        P(split),
        P(split),
        P(split),
        P(split),
        P(split),
    )
    return jax.shard_map(
        per_device,
        mesh=mesh,
        in_specs=placed,
        out_specs=(P("dp", split), P("dp", split), P("dp", split), P(None, split), P(None, split)),
        check_vma=False,
    )
```

```python
import jax
import jax.numpy as jnp
from jax import lax
from jax.experimental import pallas as pl
from jax.experimental.pallas import tpu as pltpu
from jax.sharding import PartitionSpec as P

NORM_GROUP = 512
PAIR = 128
CUTS = (2, 4)
F32 = jnp.float32
BF16 = jnp.bfloat16


def split_two(v):
    hi = v.astype(BF16)
    return hi, (v - hi.astype(F32)).astype(BF16)


def split_three(v):
    hi = v.astype(BF16)
    rest = v - hi.astype(F32)
    mid = rest.astype(BF16)
    return hi, mid, (rest - mid.astype(F32)).astype(BF16)


def dot_nn(a, b):
    return lax.dot_general(a, b, (((1,), (0,)), ((), ())), preferred_element_type=F32)


def dot_nt(a, b):
    return lax.dot_general(a, b, (((1,), (1,)), ((), ())), preferred_element_type=F32)


def dot_tn(a, b):
    return lax.dot_general(a, b, (((0,), (0,)), ((), ())), preferred_element_type=F32)


def exact_rows(rows, ones):
    n = rows.shape[0]
    got = dot_nn(jnp.concatenate(split_three(rows), axis=0), ones)
    return got[:n] + got[n : 2 * n] + got[2 * n :]


def scan_kernel(
    ends_ref, px_ref, pz_ref, pdt_ref, cot_ref, bc_ref,
    cw_ref, cb_ref, gain_ref, skipc_ref, alog_ref, dtb_ref,
    gpre_ref, gpdt_ref, gch_ref, gh_ref,
):
    block = pl.program_id(1)
    length = px_ref.shape[1]
    group = px_ref.shape[2]
    taps = cw_ref.shape[0]
    states = bc_ref.shape[2] // 2
    heads = pdt_ref.shape[2]
    head_dim = group // heads
    pairs = group // PAIR
    docs = ends_ref.shape[1]

    row = lax.broadcasted_iota(jnp.int32, (length, length), 0)
    col = lax.broadcasted_iota(jnp.int32, (length, length), 1)
    start_row = jnp.zeros((length, length), jnp.int32)
    start_col = jnp.zeros((length, length), jnp.int32)
    for k in range(docs):
        end = ends_ref[block, k]
        start_row = jnp.where(row >= end, end, start_row)
        start_col = jnp.where(col >= end, end, start_col)
    inside = (row >= col) & (start_row == start_col)
    offset = (row - start_row)[:, :PAIR]
    near = [None] + [(offset >= j).astype(F32) for j in range(1, taps)]
    low = lax.broadcasted_iota(jnp.int32, (length, PAIR), 1) < head_dim
    upto = (row <= col).astype(BF16)

    bmat = bc_ref[0, :, :states]
    cmat = bc_ref[0, :, states:]
    scores = dot_nt(cmat, bmat)

    decay = -jnp.exp(alog_ref[0])
    raw = pdt_ref[0, 0] + dtb_ref[0]
    soft = jnp.exp(-jnp.abs(raw))
    step = jnp.maximum(raw, 0.0) + jnp.log1p(soft)
    dstep = jnp.where(raw >= 0.0, 1.0, soft) / (1.0 + soft)
    level = exact_rows(step * decay, upto)
    both = jnp.concatenate(
        [step, level, jnp.zeros((length - 2 * heads, length), F32)], axis=0
    ).T

    kept = []
    square_sum = jnp.zeros((length, PAIR), F32)
    cross_sum = jnp.zeros((length, PAIR), F32)
    for k in range(pairs):
        at = slice(k * PAIR, (k + 1) * PAIR)
        x = px_ref[0, :, at]
        back = [x] + [near[j] * pltpu.roll(x, j, 0) for j in range(1, taps)]
        s = cb_ref[:, at]
        for j in range(taps):
            s = s + cw_ref[taps - 1 - j : taps - j, at] * back[j]
        sig = jax.nn.sigmoid(s)
        u = s * sig
        dsilu = sig * (1.0 + s * (1.0 - sig))
        spread = []
        for h in (2 * k, 2 * k + 1):
            gap = both[:, heads + h : heads + h + 1] - level[h : h + 1, :]
            spread.append((jnp.exp(jnp.where(inside, gap, -1e30)) * scores).astype(BF16))
        step_wide = jnp.where(low, both[:, 2 * k : 2 * k + 1], both[:, 2 * k + 1 : 2 * k + 2])
        ud = (step_wide * u).astype(BF16).astype(F32)
        zero = jnp.zeros_like(ud)
        udc = jnp.concatenate([jnp.where(low, ud, zero), jnp.where(low, zero, ud)], axis=0).astype(BF16)
        mix = dot_nn(jnp.concatenate(spread, axis=1), udc)
        y = mix + skipc_ref[:, at] * u
        z = pz_ref[0, :, at]
        zsig = jax.nn.sigmoid(z)
        zs = z * zsig
        v = y * zs
        dn = cot_ref[0, :, at].astype(F32) * gain_ref[:, at]
        square_sum = square_sum + v * v
        cross_sum = cross_sum + dn * v
        kept.append((back, u, ud, dsilu, jnp.concatenate(spread, axis=0), step_wide, mix, y, z, zsig, zs, v, dn))

    inv = lax.rsqrt(jnp.sum(square_sum, axis=1, keepdims=True) * (1.0 / group) + 1e-05)
    lean = inv * inv * jnp.sum(cross_sum, axis=1, keepdims=True) * (1.0 / group)

    channel_rows = []
    use_parts = []
    mix_parts = []
    skip_parts = []
    for k in range(pairs):
        at = slice(k * PAIR, (k + 1) * PAIR)
        back, u, ud, dsilu, spread, step_wide, mix, y, z, zsig, zs, v, dn = kept[k]
        dgain = jnp.sum(cot_ref[0, :, at].astype(F32) * (v * inv), axis=0, keepdims=True)
        dv = inv * (dn - v * lean)
        dy = dv * zs
        dz = dv * y * (zsig * (1.0 + z * (1.0 - zsig)))
        gpre_ref[1, 0, :, at] = dz.astype(BF16)
        dyr = dy.astype(BF16).astype(F32)
        zero = jnp.zeros_like(dy)
        dyc = jnp.concatenate([jnp.where(low, dyr, zero), jnp.where(low, zero, dyr)], axis=0).astype(BF16)
        turned = dot_tn(spread, dyc)
        du = step_wide * turned + skipc_ref[:, at] * dy
        use_parts.append(u * turned)
        mix_parts.append(dyr * mix - ud * turned)
        skip_parts.append(jnp.sum(dy * u, axis=0, keepdims=True))
        ds = du * dsilu
        rows = []
        dx = cw_ref[taps - 1 : taps, at] * ds
        for j in range(taps - 1, 0, -1):
            rows.append(jnp.sum(ds * back[j], axis=0, keepdims=True))
            dx = dx + cw_ref[taps - 1 - j : taps - j, at] * pltpu.roll(near[j] * ds, length - j, 0)
        rows.append(jnp.sum(ds * back[0], axis=0, keepdims=True))
        rows.append(jnp.sum(ds, axis=0, keepdims=True))
        rows.append(dgain)
        gpre_ref[0, 0, :, at] = dx.astype(BF16)
        channel_rows.append(jnp.concatenate(rows, axis=0))
    channel = jnp.concatenate(channel_rows, axis=1)

    of_head = (
        lax.broadcasted_iota(jnp.int32, (heads, group), 1) // head_dim
        == lax.broadcasted_iota(jnp.int32, (heads, group), 0)
    ).astype(BF16)
    use_hi, use_lo = split_two(jnp.concatenate(use_parts, axis=1))
    use_sum = dot_nt(of_head, use_hi) + dot_nt(of_head, use_lo)
    mix_hi, mix_lo = split_two(jnp.concatenate(mix_parts, axis=1))
    mix_sum = dot_nt(of_head, mix_hi) + dot_nt(of_head, mix_lo)
    after = exact_rows(mix_sum, (row >= col).astype(BF16))
    dalog = jnp.sum(step * after, axis=1, keepdims=True) * decay
    draw = (use_sum + decay * after) * dstep
    gpdt_ref[0, 0] = draw
    ddtb = jnp.sum(draw, axis=1, keepdims=True)
    skip_row = jnp.concatenate(skip_parts, axis=1)
    dskip = jnp.sum(jnp.where(of_head > 0, skip_row, 0.0), axis=1, keepdims=True)
    head = jnp.concatenate([dalog, ddtb, dskip], axis=1)

    @pl.when(block == 0)
    def _():
        gch_ref[...] = channel
        gh_ref[0] = head

    @pl.when(block > 0)
    def _():
        gch_ref[...] += channel
        gh_ref[0] += head


def scan_backward(ends, px, pz, pdt, cot, bc, conv_w, conv_b, norm_gain, skip_chan, a_log, dt_bias):
    blocks, length, channels = px.shape
    groups, _, heads, _ = pdt.shape
    taps = conv_w.shape[0]
    wide = channels // groups
    per_block = pl.BlockSpec((1, length, wide), lambda g, b: (b, 0, g))
    per_group = lambda rows: pl.BlockSpec((rows, wide), lambda g, b: (0, g))
    head_spec = pl.BlockSpec((1, heads, 1), lambda g, b: (g, 0, 0))
    return pl.pallas_call(
        scan_kernel,
        grid=(groups, blocks),
        in_specs=[
            pl.BlockSpec(memory_space=pltpu.SMEM),
            per_block, per_block,
            pl.BlockSpec((1, 1, heads, length), lambda g, b: (g, b, 0, 0)),
            per_block,
            pl.BlockSpec((1, length, bc.shape[2]), lambda g, b: (b, 0, 0)),
            per_group(taps), per_group(1), per_group(1), per_group(1),
            head_spec, head_spec,
        ],
        out_specs=[
            pl.BlockSpec((2, 1, length, wide), lambda g, b: (0, b, 0, g)),
            pl.BlockSpec((1, 1, heads, length), lambda g, b: (g, b, 0, 0)),
            per_group(taps + 2),
            pl.BlockSpec((1, heads, 3), lambda g, b: (g, 0, 0)),
        ],
        out_shape=[
            jax.ShapeDtypeStruct((2, blocks, length, channels), BF16),
            jax.ShapeDtypeStruct(pdt.shape, F32),
            jax.ShapeDtypeStruct((taps + 2, channels), F32),
            jax.ShapeDtypeStruct((groups, heads, 3), F32),
        ],
        compiler_params=pltpu.CompilerParams(vmem_limit_bytes=32 * 2**20),
        cost_estimate=pl.CostEstimate(
            flops=400 * blocks * length * channels,
            bytes_accessed=18 * blocks * length * channels,
            transcendentals=10 * blocks * length * channels,
        ),
    )(
        ends, px, pz, pdt, cot, bc, conv_w, conv_b[None], norm_gain[None], skip_chan[None],
        a_log.reshape(groups, heads, 1), dt_bias.reshape(groups, heads, 1),
    )


def xor_pairs(size, by):
    return [(i, i ^ by) for i in range(size)]


def shifted(shard, axis, by):
    size = lax.axis_size(axis)
    return lax.ppermute(shard, axis, [(i, (i + by) % size) for i in range(size)])


def swapped(shard, axis, by):
    return lax.ppermute(shard, axis, xor_pairs(lax.axis_size(axis), by))


def after(value, *others):
    return lax.optimization_barrier((value, *others))[0]


def tree_sum(parts):
    while len(parts) > 1:
        parts = [a + b for a, b in zip(parts[0::2], parts[1::2], strict=True)]
    return parts[0]


def per_device(
    tokens,
    send_flags,
    doc_lengths,
    cotangent,
    w_x,
    w_z,
    w_dt,
    w_bc,
    conv_w,
    conv_b,
    norm_gain,
    a_log,
    dt_bias,
    skip_scale,
):
    dp_count = lax.axis_size("dp")
    fsdp_count = lax.axis_size("fsdp")
    pair_count = lax.axis_size("tensor")
    dp_index = lax.axis_index("dp")
    column = lax.axis_index("fsdp")
    member = lax.axis_index("tensor")
    slots, length, width = tokens.shape
    half = length // pair_count
    chan = w_x.shape[1]
    head_count = w_dt.shape[1]
    groups = chan // NORM_GROUP
    taps = conv_w.shape[0]
    piece = width // dp_count
    zero = jnp.zeros((), jnp.int32)

    before = (dp_index + dp_count - 1) % dp_count
    earlier = (dp_index + dp_count - 2) % dp_count
    came = send_flags[before, column] == 1
    own_send = 1 - send_flags[before, column]

    def in_order(mine, other):
        first = jnp.where(member == 0, mine, other)
        second = jnp.where(member == 0, other, mine)
        return jnp.concatenate((first, second), axis=-2)

    def across(own):
        held = [own]
        for k in range(1, fsdp_count):
            low = k & -k
            held.append(swapped(held[k ^ low], "fsdp", low))
        return held

    def half_rows(slot):
        return lax.dynamic_slice(tokens, (slot, member * half, zero), (1, half, width))[0]

    mine_x = jnp.where(came, shifted(half_rows(own_send), "dp", 1), half_rows(zero))
    mine = [mine_x]
    for k in range(1, fsdp_count):
        low = k & -k
        mine.append(swapped(after(mine[k ^ low], mine[low // 2]), "fsdp", low))
    other = [swapped(part, "tensor", 1) for part in mine]
    x_blocks = [in_order(part, rest) for part, rest in zip(mine, other, strict=True)]

    held_d = after(cotangent, mine_x)

    def slabs(slot):
        return jnp.stack(
            [
                lax.dynamic_slice(held_d, (slot, zero, (f * pair_count + member) * chan), (1, length, chan))[0]
                for f in range(fsdp_count)
            ]
        )

    mine_d = jnp.where(came, shifted(slabs(own_send), "dp", 1), slabs(zero))
    d_blocks = []
    for k in range(fsdp_count):
        part = lax.dynamic_index_in_dim(mine_d, column ^ k, 0, keepdims=False)
        part = after(part, mine[k]) if k > 1 else part
        d_blocks.append(swapped(part, "fsdp", k) if k else part)

    def columns_for(rows, m):
        at = (zero,) * (rows.ndim - 1) + ((dp_index ^ m) * piece,)
        return lax.dynamic_slice(rows, at, rows.shape[:-1] + (piece,))

    far_x = jnp.stack([swapped(columns_for(mine_x, m), "dp", m) for m in range(2, dp_count)])
    far_x = jnp.stack(across(after(far_x, other[-1], d_blocks[-1])))
    far_x = in_order(far_x, swapped(far_x, "tensor", 1))

    columns = column ^ jnp.arange(fsdp_count, dtype=jnp.int32)
    picks = jnp.where(
        send_flags[before][columns] == 1,
        (before * fsdp_count + columns) * slots + 1 - send_flags[earlier][columns],
        (dp_index * fsdp_count + columns) * slots,
    )
    sizes = doc_lengths[picks]
    ends = [sizes[:, 0]]
    for k in range(1, sizes.shape[1] - 1):
        ends.append(ends[-1] + sizes[:, k])
    ends = jnp.stack(ends, axis=1)
    skip_chan = jnp.repeat(skip_scale, chan // head_count)

    cuts = [0] + [fsdp_count * part // 4 for part in CUTS]
    x_parts = [[] for _ in range(dp_count)]
    g_parts = [[] for _ in range(dp_count)]
    dt_parts = []
    partner_cols = []
    channel_parts = []
    head_parts = []
    for first, last in zip(cuts, cuts[1:]):
        per_chunk = last - first
        xs = jnp.concatenate(x_blocks[first:last], axis=0)
        cot = jnp.stack(d_blocks[first:last])
        px = jnp.dot(xs, w_x, preferred_element_type=F32).reshape(per_chunk, length, chan)
        pz = jnp.dot(xs, w_z, preferred_element_type=F32).reshape(per_chunk, length, chan)
        bc = jnp.dot(xs, w_bc, preferred_element_type=F32).astype(BF16)
        bc = bc.reshape(per_chunk, length, w_bc.shape[1])
        pdt = lax.dot_general(w_dt, xs, (((0,), (1,)), ((), ())), preferred_element_type=F32)
        pdt = pdt.reshape(groups, head_count // groups, per_chunk, length).transpose(0, 2, 1, 3)
        x_parts[0].append(columns_for(xs, 0))
        partner_cols.append(columns_for(xs, 1))
        if last == fsdp_count:
            x_parts[1].append(swapped(jnp.concatenate(partner_cols, axis=0), "dp", 1))
        due = [g_parts[1][-1]] if first else []
        gpre, gpdt, gch, gh = scan_backward(
            ends[first:last], px, pz, pdt, cot, bc,
            conv_w, conv_b, norm_gain, after(skip_chan, *due), a_log, dt_bias,
        )
        dt_parts.append(gpdt.transpose(1, 0, 2, 3).reshape(per_chunk, head_count, length))
        channel_parts.append(gch)
        head_parts.append(gh)
        gpre = gpre.reshape(2, per_chunk * length, chan)
        for m in range(0, dp_count, 2):
            g_parts[m].append(swapped(gpre, "dp", m) if m else gpre)
            g_parts[m + 1].append(swapped(g_parts[m][-1], "dp", 1))
        for m in range(2, dp_count):
            x_parts[m].append(far_x[first:last, m - 2].reshape(-1, piece))

    gpdt = jnp.concatenate(dt_parts, axis=0).reshape(-1, chan)
    rows = [gpdt, sum(channel_parts[1:], channel_parts[0])]
    heads = sum(head_parts[1:], head_parts[0]).reshape(head_count, 3).T
    rows.append(jnp.pad(heads.reshape(1, -1), ((0, 0), (0, chan - 3 * head_count))))
    packed = jnp.concatenate(rows, axis=0)
    packed = after(packed, g_parts[1][-1])
    packs = jnp.stack([packed] + [swapped(packed, "dp", m) for m in range(2, dp_count, 2)])
    packs = jnp.stack((packs, swapped(packs, "dp", 1)), axis=1).reshape((dp_count,) + packed.shape)
    dt_rows = gpdt.shape[0]
    small = tree_sum([packs[m, dt_rows:] for m in range(dp_count)])
    channel_sum = small[: taps + 2]
    head_sum = small[taps + 2, : 3 * head_count].reshape(3, head_count)

    dt_all = packs[:, :dt_rows].reshape(dp_count * fsdp_count, head_count, length)
    dt_all = dt_all.astype(BF16).transpose(1, 0, 2).reshape(head_count, -1)
    def product(ms, which):
        x_all = jnp.concatenate([p for m in ms for p in x_parts[m]], axis=0)
        g_all = jnp.concatenate([p[which] for m in ms for p in g_parts[m]], axis=0)
        return lax.dot_general(x_all, g_all, (((0,), (0,)), ((), ())), preferred_element_type=F32)

    near, far = tuple(range(2)), tuple(range(2, dp_count))
    grad_x = product(near, 0) + product(far, 0)
    grad_z = product(near, 1) + product(far, 1)
    x_all = jnp.concatenate([p for parts in x_parts for p in parts], axis=0)
    grad_dt = lax.dot_general(x_all, dt_all, (((0,), (1,)), ((), ())), preferred_element_type=F32)
    return grad_x, grad_z, grad_dt, channel_sum, head_sum


def solution(mesh):
    split = ("fsdp", "tensor")
    placed = (
        P(("dp", "fsdp"), None, None),
        P(),
        P(),
        P(("dp", "fsdp"), None, None),
        P(None, split),
        P(None, split),
        P(None, split),
        P(),
        P(None, split),
        P(split),
        P(split),
        P(split),
        P(split),
        P(split),
    )
    return jax.shard_map(
        per_device,
        mesh=mesh,
        in_specs=placed,
        out_specs=(P("dp", split), P("dp", split), P("dp", split), P(None, split), P(None, split)),
        check_vma=False,
    )
```
